256 devices in a mesh: frame: 64 (over z, y, core), sector: 4 (over x).
Axes of the slice: x: 4, y: 4, z: 8, core: 2. Of those that a mesh axis runs over, the one named last changes fastest.
Arguments:
- intensity: bfloat16 [1024, 786432], P(('frame', 'sector')), may hold values from 0.099609375 to 10
- block_annulus: int32 [4, 1536], P('sector', 'frame'), may hold values from 0 to 255, as said below
Outputs:
- correlation: float32 [4, 64, 1024, 1024], P('sector', 'frame')
The draws below stay inside these ranges and needn't reach their ends.
Inputs may be any that keep to these rules, and one draw needn't show every extreme that they name: `block_annulus`: annuli 2k and 2k + 1 together fill the blocks 2k * 24 to (2k + 2) * 24 - 1 of the flattened table, annulus 2k first; every annulus holds 1 to 47 blocks, and some annulus holds exactly 47.
All inputs are finite; a program needn't handle non-finite values.
Results may differ from the reference program's by a relative error of at most 0.0003.
Values may be sent and summed in bfloat16 or wider, within the bound.
No kernel may reach another device: no remote copies, remote signals or barrier semaphores. Data moves between devices by JAX's collectives and lax.ppermute only.
A program may use at most 128 MiB of HBM per device.

```python
import math
import jax
import jax.numpy as jnp
from jax import lax

F = 1024
BLOCKS_DEV = 24
PIX_DEV = 3072
PIXELS = 786432
ANNULI = 256
N_SECTOR = 4
DEVICES = 256


def draw_block_annulus(key, part):
    key = jax.random.fold_in(key, 5)
    first_key, second_key = jax.random.split(key)
    pair_total = DEVICES // 2
    offset_shift = jax.random.randint(first_key, (pair_total,), -(BLOCKS_DEV - 1), BLOCKS_DEV)
    chosen = jax.random.randint(second_key, (), 0, pair_total)
    offset_shift = jnp.where(jnp.arange(pair_total) == chosen, BLOCKS_DEV - 1, offset_shift)
    block_index = jnp.arange(DEVICES * BLOCKS_DEV, dtype=jnp.int32)
    pair_of_block = block_index // (2 * BLOCKS_DEV)
    inside = block_index % (2 * BLOCKS_DEV)
    second = (inside >= BLOCKS_DEV + offset_shift[pair_of_block]).astype(jnp.int32)
    return (2 * pair_of_block + second).reshape(N_SECTOR, -1)


def shard_levels(rng, extent, cuts, least, largest):
    factor_of, own = 1.0, jax.random.fold_in(rng, 6)
    for dim, parts in cuts:
        heights = jnp.exp(jax.random.uniform(jax.random.fold_in(own, dim), (parts,), jnp.float32, least / len(cuts), largest / len(cuts)))
        factor_of = factor_of * jnp.repeat(heights, extent[dim] // parts).reshape([-1 if axis == dim else 1 for axis in range(len(extent))])
    return factor_of


def setup_inputs(seed: int = 0) -> dict:
    key_of = jax.random.split(jax.random.key(seed), 3)
    intensity = jnp.clip(jnp.exp(math.log(10.0) - 4.609084 * jax.random.uniform(key_of[0], (F, PIXELS), jnp.float32) ** shard_levels(key_of[0], (F, PIXELS), ((0, 256),), -0.2, 0.2)), 0.099609375, 10.0).astype(jnp.bfloat16)
    block_annulus = draw_block_annulus(jax.random.fold_in(key_of[2], 71), 0)
    return dict(intensity=intensity, block_annulus=block_annulus)


def reference(intensity, block_annulus):
    annulus_blocks = block_annulus.reshape(-1)
    frames = intensity.shape[0]
    pair_cols = 2 * PIX_DEV
    def one_pair(pair_index):
        window = lax.dynamic_slice_in_dim(intensity, pair_index * pair_cols, pair_cols, 1)
        blocks = lax.dynamic_slice_in_dim(annulus_blocks, pair_index * (2 * BLOCKS_DEV), 2 * BLOCKS_DEV, 0)
        pixel_annulus = jnp.repeat(blocks, 128)
        def one_annulus(annulus_number):
            flags = (pixel_annulus == annulus_number).astype(intensity.dtype)
            masked = window * flags[None, :]
            gram = lax.dot_general(masked, window, (((1,), (1,)), ((), ())), preferred_element_type=jnp.float32)
            annulus_sums = jnp.dot(window, flags, preferred_element_type=jnp.float32)
            pixel_count = 128.0 * jnp.sum((blocks == annulus_number).astype(jnp.float32))
            return pixel_count * gram / (annulus_sums[:, None] * annulus_sums[None, :])
        return jnp.stack([one_annulus(2 * pair_index), one_annulus(2 * pair_index + 1)])
    result = lax.map(one_pair, jnp.arange(ANNULI // 2, dtype=jnp.int32))
    return result.reshape(N_SECTOR, ANNULI // N_SECTOR, frames, frames)
```

```python
import jax
import jax.numpy as jnp
from jax import lax
from jax.experimental import pallas as pl
from jax.experimental.pallas import tpu as pltpu
from jax.sharding import PartitionSpec as P

FRAMES = 1024
TILE = 256
PARTS = FRAMES // TILE
HEAD = 16
BLOCKS = 24
QUAD = 4
WIDTH = 128 * QUAD
STARTS = tuple(sum(HEAD + TILE * (k + 1) for k in range(j)) for j in range(PARTS + 1))
ROWS = STARTS[PARTS]


def gram_kernel(number_ref, annulus_ref, got_ref, own_ref, other_ref, ordered, masked):
    my_annulus = number_ref[0]
    own_ref[...] = jnp.zeros_like(own_ref)
    other_ref[...] = jnp.zeros_like(other_ref)
    target = lax.broadcasted_iota(jnp.int32, (TILE, TILE), 0)
    source = lax.broadcasted_iota(jnp.int32, (TILE, TILE), 1)
    wanted = (
        ((target >> 2) & 3) * 64
        + ((target >> 4) & 3) * 16
        + (target >> 6) * 4
        + (target & 3)
    )
    order = jnp.where(source == wanted, 1.0, 0.0).astype(jnp.bfloat16)
    lane_block = lax.broadcasted_iota(jnp.int32, (HEAD, WIDTH), 1) // 128

    def two_quads(pair, carry):
        for g in range(FRAMES // 64):
            halves = [
                got_ref[:, 4 * g : 4 * g + 4, 2 * pair + h].reshape(TILE, 128)
                for h in range(2)
            ]
            moved = lax.dot_general(
                order,
                jnp.concatenate(halves, axis=1),
                (((1,), (0,)), ((), ())),
                preferred_element_type=jnp.float32,
            ).astype(jnp.bfloat16)
            for h in range(2):
                for b in range(QUAD):
                    ordered[h, 64 * g : 64 * g + 64, 128 * b : 128 * b + 128] = (
                        moved[64 * b : 64 * b + 64, 128 * h : 128 * h + 128]
                    )

        def quad(h, carry):
            first = QUAD * (2 * pair + h)
            flags = [(annulus_ref[0, first + b] == my_annulus).astype(jnp.int32) for b in range(QUAD)]
            own_here = flags[0] + flags[1] + flags[2] + flags[3]
            own_lanes = jnp.zeros((HEAD, WIDTH), jnp.int32)
            for b in range(QUAD):
                own_lanes = jnp.where(lane_block == b, flags[b], own_lanes)

            def part(lanes, out_ref):
                mask = lanes.astype(jnp.float32).astype(jnp.bfloat16)
                masked[0:HEAD] = mask
                masked[HEAD:] = ordered[h] * mask[0:1]
                for j in range(PARTS):
                    rows = HEAD + TILE * (j + 1)
                    out_ref[STARTS[j] : STARTS[j] + rows] += lax.dot_general(
                        masked[0:rows],
                        ordered[h, TILE * j : TILE * j + TILE],
                        (((1,), (1,)), ((), ())),
                        preferred_element_type=jnp.float32,
                    )

            @pl.when(own_here > 0)
            def _():
                part(own_lanes, own_ref)

            @pl.when(own_here < QUAD)
            def _():
                part(1 - own_lanes, other_ref)

            return carry

        return lax.fori_loop(0, 2, quad, carry)

    lax.fori_loop(0, BLOCKS // QUAD // 2, two_quads, 0)
    own_blocks = jnp.int32(0)
    for b in range(BLOCKS):
        own_blocks += (annulus_ref[0, b] == my_annulus).astype(jnp.int32)
    own_count = 128.0 * own_blocks.astype(jnp.float32)
    own_ref[8:16] = jnp.full((8, TILE), own_count, jnp.float32)
    other_ref[8:16] = jnp.full((8, TILE), 128.0 * BLOCKS - own_count, jnp.float32)


def finish_kernel(own_ref, got_ref, out_ref):
    step = pl.program_id(0)

    def total(start, rows):
        return own_ref[start : start + rows] + got_ref[start : start + rows]

    inverse = [1.0 / total(STARTS[j], 8)[0:1] for j in range(PARTS)]
    count = total(8, 8)[0:1]

    def column(j):
        return jnp.concatenate(
            [
                jnp.transpose(jnp.broadcast_to(inverse[j][:, 128 * k : 128 * k + 128], (128, 128)))
                for k in range(TILE // 128)
            ],
            axis=0,
        )

    for i in range(PARTS):

        @pl.when(step == i)
        def _(i=i):
            left = column(i)
            left = jnp.concatenate([left, left], axis=1)
            for j in range(PARTS):
                low, high = min(i, j), max(i, j)
                block = total(STARTS[high] + HEAD + TILE * low, TILE)
                if j < i:
                    block = jnp.transpose(block)
                out_ref[:, TILE * j : TILE * j + TILE] = block * left * (count * inverse[j])


def packed_grams(number, block_annulus, arrived):
    shape = jax.ShapeDtypeStruct((ROWS, TILE), jnp.float32)
    vmem = pl.BlockSpec(memory_space=pltpu.VMEM)
    smem = pl.BlockSpec(memory_space=pltpu.SMEM)
    return pl.pallas_call(
        gram_kernel,
        out_shape=(shape, shape),
        in_specs=[smem, smem, vmem],
        out_specs=(vmem, vmem),
        scratch_shapes=[
            pltpu.VMEM((2, FRAMES, WIDTH), jnp.bfloat16),
            pltpu.VMEM((HEAD + FRAMES, WIDTH), jnp.bfloat16),
        ],
        compiler_params=pltpu.CompilerParams(vmem_limit_bytes=40 << 20),
        name="grams",
    )(number, block_annulus, arrived)


def finished(own, got):
    whole = pl.BlockSpec((ROWS, TILE), lambda i: (0, 0))
    return pl.pallas_call(
        finish_kernel,
        grid=(PARTS,),
        out_shape=jax.ShapeDtypeStruct((FRAMES, FRAMES), jnp.float32),
        in_specs=[whole, whole],
        out_specs=pl.BlockSpec((TILE, FRAMES), lambda i: (i, 0)),
        compiler_params=pltpu.CompilerParams(vmem_limit_bytes=40 << 20),
        name="finish",
    )(own, got)


def local(intensity, block_annulus):
    devices = lax.axis_size("sector") * lax.axis_size("frame")
    pieces = intensity.reshape(4, devices, BLOCKS, 128).transpose(1, 2, 0, 3)
    arrived = lax.all_to_all(pieces, ("sector", "frame"), split_axis=0, concat_axis=0, tiled=True)
    arrived = arrived.reshape(4, devices // 4, BLOCKS // QUAD, 4 * QUAD, 128)
    my_annulus = lax.axis_index("sector") * lax.axis_size("frame") + lax.axis_index("frame")
    own, other = packed_grams(my_annulus.reshape(1).astype(jnp.int32), block_annulus, arrived)
    pairs = [(source, source ^ 1) for source in range(lax.axis_size("frame"))]
    got = lax.ppermute(other, "frame", pairs)
    return finished(own, got).reshape(1, 1, FRAMES, FRAMES)


def solution(mesh):
    in_specs = (P(("frame", "sector"), None), P("sector", "frame"))
    out_specs = P("sector", "frame", None, None)
    return jax.shard_map(local, mesh=mesh, in_specs=in_specs, out_specs=out_specs, check_vma=False)
```

```python
import functools

import jax
import jax.numpy as jnp
from jax import lax
from jax.experimental import pallas as pl
from jax.experimental.pallas import tpu as pltpu
from jax.sharding import PartitionSpec as P

FRAMES = 1024
TILE = 256
PARTS = FRAMES // TILE
HEAD = 16
BLOCKS = 24
QUAD = 4
WIDTH = 128 * QUAD
CHUNKS = BLOCKS // (2 * QUAD)
GROUPS = ((0, 1, 2), (3,))
ALL = tuple(range(PARTS))
VMEM = pl.BlockSpec(memory_space=pltpu.VMEM)
SMEM = pl.BlockSpec(memory_space=pltpu.SMEM)
ANY = pl.BlockSpec(memory_space=pl.ANY)


def starts_of(panels):
    starts, row = {}, 0
    for j in panels:
        starts[j] = row
        row += HEAD + TILE * (j + 1)
    return starts, row


def put_in_order(landed, ordered, chunk, flags):
    target = lax.broadcasted_iota(jnp.int32, (TILE, TILE), 0)
    source = lax.broadcasted_iota(jnp.int32, (TILE, TILE), 1)
    wanted = (
        ((target >> 2) & 3) * 64
        + ((target >> 4) & 3) * 16
        + (target >> 6) * 4
        + (target & 3)
    )
    order = jnp.where(source == wanted, 1.0, 0.0).astype(jnp.bfloat16)
    keep = [flag.astype(jnp.float32) for flag in flags]
    ordered[chunk, 0:HEAD] = jnp.ones((HEAD, 2 * WIDTH), jnp.bfloat16)
    for g in range(FRAMES // 64):
        rows = [landed[:, 4 * g : 4 * g + 4, 2 * chunk + h].reshape(TILE, 128) for h in range(2)]
        moved = lax.dot_general(
            order,
            jnp.concatenate(rows, axis=1),
            (((1,), (0,)), ((), ())),
            preferred_element_type=jnp.float32,
        )
        for h in range(2):
            for b in range(QUAD):
                lane = WIDTH * h + 128 * b
                block = moved[64 * b : 64 * b + 64, 128 * h : 128 * h + 128]
                ordered[chunk, HEAD + 64 * g : HEAD + 64 * g + 64, lane : lane + 128] = (
                    block * keep[QUAD * h + b]
                ).astype(jnp.bfloat16)


def gram_kernel(own, panels, arrives, annulus_ref, *refs):
    if arrives:
        landed, out_ref, ordered = refs
    else:
        ordered, out_ref = refs
    starts, _ = starts_of(panels)
    number = lax.axis_index("sector") * lax.axis_size("frame") + lax.axis_index("frame")

    def chosen(block):
        same = annulus_ref[0, block] == number
        return jnp.where(same, 1, 0) if own else jnp.where(same, 0, 1)

    out_ref[...] = jnp.zeros_like(out_ref)
    flags = [chosen(b) for b in range(BLOCKS)]
    total = sum(flags[1:], flags[0])

    def products(chunk):
        for j in panels:
            rows = HEAD + TILE * (j + 1)
            out_ref[starts[j] : starts[j] + rows] += lax.dot_general(
                ordered[chunk, 0:rows],
                ordered[chunk, HEAD + TILE * j : HEAD + TILE * j + TILE],
                (((1,), (1,)), ((), ())),
                preferred_element_type=jnp.float32,
            )

    def one_chunk(chunk):
        if arrives:
            here = flags[2 * QUAD * chunk : 2 * QUAD * (chunk + 1)]
            put_in_order(landed, ordered, chunk, here)
        products(chunk)

    if own:
        for chunk in range(CHUNKS):
            here = flags[2 * QUAD * chunk : 2 * QUAD * (chunk + 1)]
            pl.when(sum(here[1:], here[0]) > 0)(functools.partial(one_chunk, chunk))
    else:

        @pl.when(total > 0)
        def _():
            for chunk in range(CHUNKS):
                one_chunk(chunk)

    out_ref[8:16] = jnp.full((8, TILE), 128.0 * total.astype(jnp.float32), jnp.float32)


def packed_gram(own, panels, block_annulus, operand):
    arrives = operand.ndim == 5
    packed = jax.ShapeDtypeStruct((starts_of(panels)[1], TILE), jnp.float32)
    in_order = (CHUNKS, HEAD + FRAMES, 2 * WIDTH)
    scratch = []
    out_shape, out_specs = packed, VMEM
    if arrives:
        if own:
            scratch = [pltpu.VMEM(in_order, jnp.bfloat16)] + scratch
        else:
            out_shape = (packed, jax.ShapeDtypeStruct(in_order, jnp.bfloat16))
            out_specs = (VMEM, VMEM)
    return pl.pallas_call(
        functools.partial(gram_kernel, own, panels, arrives),
        out_shape=out_shape,
        in_specs=[SMEM, VMEM],
        out_specs=out_specs,
        scratch_shapes=scratch,
        compiler_params=pltpu.CompilerParams(vmem_limit_bytes=(24 if arrives else 6) << 20),
        cost_estimate=pl.CostEstimate(
            flops=2 * packed.size * 128 * BLOCKS, bytes_accessed=6 << 20, transcendentals=0
        ),
        name="own_gram" if own else "other_gram",
    )(block_annulus, operand)


def finish_kernel(panels, known, groups, own_ref, *refs):
    got_refs, refs = refs[:groups], refs[groups:]
    out_ref, corner, edge, copied = refs[-4:]
    own_starts, _ = starts_of(ALL)
    place = {
        j: (got_refs[g], starts_of(GROUPS[g])[0][j]) for g in range(groups) for j in GROUPS[g]
    }

    def total(j, row, rows):
        got_ref, start = place[j]
        return (
            own_ref[own_starts[j] + row : own_starts[j] + row + rows]
            + got_ref[start + row : start + row + rows]
        )

    inverse = {j: 1.0 / total(j, 0, 8)[0:1] for j in known}
    count = total(0, 8, 8)[0:1]

    def column(j):
        half = [
            jnp.transpose(jnp.broadcast_to(inverse[j][:, 128 * k : 128 * k + 128], (128, 128)))
            for k in range(TILE // 128)
        ]
        half = jnp.concatenate(half, axis=0)
        return jnp.concatenate([half, half], axis=1)

    left = {j: column(j) for j in known}
    copies = []
    for j in panels:
        for i in range(j + 1):
            block = total(j, HEAD + TILE * i, TILE) * left[i] * (count * inverse[j])
            column_of = slice(TILE * j, TILE * j + TILE)
            if i < j:
                edge[TILE * i : TILE * i + TILE, column_of] = block
                copies.append(
                    pltpu.make_async_copy(
                        edge.at[TILE * i : TILE * i + TILE, column_of],
                        out_ref.at[TILE * i : TILE * i + TILE, column_of],
                        copied.at[len(copies)],
                    )
                )
                copies[-1].start()
                block = jnp.transpose(block)
            corner[column_of, TILE * i : TILE * i + TILE] = block
        rows = slice(TILE * j, TILE * j + TILE)
        copies.append(
            pltpu.make_async_copy(
                corner.at[rows, 0 : TILE * (j + 1)],
                out_ref.at[rows, 0 : TILE * (j + 1)],
                copied.at[len(copies)],
            )
        )
        copies[-1].start()
    for copy in copies:
        copy.wait()


def finished(own, got):
    out = None
    for g, panels in enumerate(GROUPS):
        known = tuple(range(panels[-1] + 1))
        operands = [own, *got[: g + 1]] + ([] if out is None else [out])
        copies = sum(j + 1 for j in panels)
        out = pl.pallas_call(
            functools.partial(finish_kernel, panels, known, g + 1),
            out_shape=jax.ShapeDtypeStruct((FRAMES, FRAMES), jnp.float32),
            in_specs=[VMEM] * (g + 2) + ([] if out is None else [ANY]),
            out_specs=ANY,
            input_output_aliases={} if out is None else {g + 2: 0},
            scratch_shapes=[
                pltpu.VMEM((FRAMES, FRAMES), jnp.float32),
                pltpu.VMEM((FRAMES, FRAMES), jnp.float32),
                pltpu.SemaphoreType.DMA((copies,)),
            ],
            compiler_params=pltpu.CompilerParams(vmem_limit_bytes=12 << 20),
            cost_estimate=pl.CostEstimate(
                flops=8 << 20, bytes_accessed=4 * TILE * TILE * copies * 2, transcendentals=0
            ),
            name="finish",
        )(*operands)
    return out


def local(intensity, block_annulus):
    devices = lax.axis_size("sector") * lax.axis_size("frame")
    pieces = intensity.reshape(4, devices, BLOCKS, 128).transpose(1, 2, 0, 3)
    arrived = lax.all_to_all(pieces, ("sector", "frame"), split_axis=0, concat_axis=0, tiled=True)
    arrived = arrived.reshape(4, devices // 4, BLOCKS // QUAD, 4 * QUAD, 128)
    pairs = [(source, source ^ 1) for source in range(lax.axis_size("frame"))]
    got, pixels = [], arrived
    for panels in GROUPS:
        other = packed_gram(False, panels, block_annulus, pixels)
        if not got:
            other, pixels = other
        got.append(lax.ppermute(other, "frame", pairs))
    own = packed_gram(True, ALL, block_annulus, arrived)
    return finished(own, got).reshape(1, 1, FRAMES, FRAMES)


def solution(mesh):
    in_specs = (P(("frame", "sector"), None), P("sector", "frame"))
    out_specs = P("sector", "frame", None, None)
    return jax.shard_map(local, mesh=mesh, in_specs=in_specs, out_specs=out_specs, check_vma=False)
```

```python
import functools

import jax
import jax.numpy as jnp
from jax import lax
from jax.experimental import pallas as pl
from jax.experimental.pallas import tpu as pltpu
from jax.sharding import PartitionSpec as P

FRAMES = 1024
TILE = 256
PARTS = FRAMES // TILE
HEAD = 16
BLOCKS = 24
QUAD = 4
WIDTH = 128 * QUAD
CHUNKS = BLOCKS // (2 * QUAD)
GROUPS = ((0, 1, 2), (3,))
VMEM = pl.BlockSpec(memory_space=pltpu.VMEM)
SMEM = pl.BlockSpec(memory_space=pltpu.SMEM)
ANY = pl.BlockSpec(memory_space=pl.ANY)


def starts_of(panels):
    starts, row = {}, 0
    for j in panels:
        starts[j] = row
        row += HEAD + TILE * (j + 1)
    return starts, row


def put_in_order(landed, ordered, chunk):
    target = lax.broadcasted_iota(jnp.int32, (TILE, TILE), 0)
    source = lax.broadcasted_iota(jnp.int32, (TILE, TILE), 1)
    wanted = (
        ((target >> 2) & 3) * 64
        + ((target >> 4) & 3) * 16
        + (target >> 6) * 4
        + (target & 3)
    )
    order = jnp.where(source == wanted, 1.0, 0.0).astype(jnp.bfloat16)
    ordered[chunk, 0:HEAD] = jnp.ones((HEAD, 2 * WIDTH), jnp.bfloat16)
    for g in range(FRAMES // 64):
        rows = [landed[:, 4 * g : 4 * g + 4, 2 * chunk + h].reshape(TILE, 128) for h in range(2)]
        moved = lax.dot_general(
            order,
            jnp.concatenate(rows, axis=1),
            (((1,), (0,)), ((), ())),
            preferred_element_type=jnp.float32,
        ).astype(jnp.bfloat16)
        for h in range(2):
            for b in range(QUAD):
                lane = WIDTH * h + 128 * b
                ordered[chunk, HEAD + 64 * g : HEAD + 64 * g + 64, lane : lane + 128] = moved[
                    64 * b : 64 * b + 64, 128 * h : 128 * h + 128
                ]


def gram_kernel(panels, arrives, annulus_ref, *refs):
    if arrives:
        landed, own_ref, other_ref, ordered, masked = refs
    else:
        ordered, own_ref, other_ref, masked = refs
    starts, _ = starts_of(panels)
    number = lax.axis_index("sector") * lax.axis_size("frame") + lax.axis_index("frame")
    own_ref[...] = jnp.zeros_like(own_ref)
    other_ref[...] = jnp.zeros_like(other_ref)
    lane_block = lax.broadcasted_iota(jnp.int32, (HEAD, WIDTH), 1) // 128
    flags = [jnp.where(annulus_ref[0, b] == number, 1, 0) for b in range(BLOCKS)]

    def add_products(out_ref, left_ref, chunk, lane, width):
        for j in panels:
            rows = HEAD + TILE * (j + 1)
            out_ref[starts[j] : starts[j] + rows] += lax.dot_general(
                left_ref[0:rows],
                ordered[chunk, HEAD + TILE * j : HEAD + TILE * j + TILE, lane : lane + width],
                (((1,), (1,)), ((), ())),
                preferred_element_type=jnp.float32,
            )

    def one_quad(out_ref, chunk, h, chosen):
        lanes = jnp.zeros((HEAD, WIDTH), jnp.int32)
        for b in range(QUAD):
            lanes = jnp.where(lane_block == b, chosen[b], lanes)
        mask = lanes.astype(jnp.float32).astype(jnp.bfloat16)
        last = HEAD + TILE * (panels[-1] + 1)
        masked[0:last] = ordered[chunk, 0:last, WIDTH * h : WIDTH * h + WIDTH] * mask[0:1]
        add_products(out_ref, masked, chunk, WIDTH * h, WIDTH)

    for chunk in range(CHUNKS):
        if arrives:
            put_in_order(landed, ordered, chunk)
        here = flags[2 * QUAD * chunk : 2 * QUAD * (chunk + 1)]
        owned = sum(here[1:], here[0])
        for out_ref, all_here in ((own_ref, 2 * QUAD), (other_ref, 0)):
            pl.when(owned == all_here)(
                functools.partial(add_products, out_ref, ordered.at[chunk], chunk, 0, 2 * WIDTH)
            )

        @pl.when((owned > 0) & (owned < 2 * QUAD))
        def _(chunk=chunk, here=here):
            for h in range(2):
                quad = here[QUAD * h : QUAD * h + QUAD]
                for out_ref, chosen in ((own_ref, quad), (other_ref, [1 - f for f in quad])):
                    pl.when(sum(chosen[1:], chosen[0]) > 0)(
                        functools.partial(one_quad, out_ref, chunk, h, chosen)
                    )

    count = 128.0 * sum(flags[1:], flags[0]).astype(jnp.float32)
    own_ref[8:16] = jnp.full((8, TILE), count, jnp.float32)
    other_ref[8:16] = jnp.full((8, TILE), 128.0 * BLOCKS - count, jnp.float32)


def packed_grams(panels, block_annulus, operand):
    arrives = operand.ndim == 5
    packed = jax.ShapeDtypeStruct((starts_of(panels)[1], TILE), jnp.float32)
    in_order = jax.ShapeDtypeStruct((CHUNKS, HEAD + FRAMES, 2 * WIDTH), jnp.bfloat16)
    out_shape = (packed, packed, in_order) if arrives else (packed, packed)
    return pl.pallas_call(
        functools.partial(gram_kernel, panels, arrives),
        out_shape=out_shape,
        in_specs=[SMEM, VMEM],
        out_specs=(VMEM,) * len(out_shape),
        scratch_shapes=[pltpu.VMEM((HEAD + FRAMES, WIDTH), jnp.bfloat16)],
        compiler_params=pltpu.CompilerParams(vmem_limit_bytes=24 << 20),
        cost_estimate=pl.CostEstimate(
            flops=2 * packed.size * 128 * BLOCKS, bytes_accessed=6 << 20, transcendentals=0
        ),
        name="grams",
    )(block_annulus, operand)


def finish_kernel(panels, known, groups, *refs):
    own_refs, got_refs, refs = refs[:groups], refs[groups : 2 * groups], refs[2 * groups :]
    out_ref, corner, edge, copied = refs[-4:]
    place = {
        j: (own_refs[g], got_refs[g], starts_of(GROUPS[g])[0][j])
        for g in range(groups)
        for j in GROUPS[g]
    }

    def total(j, row, rows):
        own_ref, got_ref, start = place[j]
        return own_ref[start + row : start + row + rows] + got_ref[start + row : start + row + rows]

    inverse = {j: 1.0 / total(j, 0, 8)[0:1] for j in known}
    count = total(0, 8, 8)[0:1]

    def column(j):
        half = [
            jnp.transpose(jnp.broadcast_to(inverse[j][:, 128 * k : 128 * k + 128], (128, 128)))
            for k in range(TILE // 128)
        ]
        half = jnp.concatenate(half, axis=0)
        return jnp.concatenate([half, half], axis=1)

    left = {j: column(j) for j in known}
    copies = []
    for j in panels:
        for i in range(j + 1):
            block = total(j, HEAD + TILE * i, TILE) * left[i] * (count * inverse[j])
            column_of = slice(TILE * j, TILE * j + TILE)
            if i < j:
                edge[TILE * i : TILE * i + TILE, column_of] = block
                copies.append(
                    pltpu.make_async_copy(
                        edge.at[TILE * i : TILE * i + TILE, column_of],
                        out_ref.at[TILE * i : TILE * i + TILE, column_of],
                        copied.at[len(copies)],
                    )
                )
                copies[-1].start()
                block = jnp.transpose(block)
            corner[column_of, TILE * i : TILE * i + TILE] = block
        rows = slice(TILE * j, TILE * j + TILE)
        copies.append(
            pltpu.make_async_copy(
                corner.at[rows, 0 : TILE * (j + 1)],
                out_ref.at[rows, 0 : TILE * (j + 1)],
                copied.at[len(copies)],
            )
        )
        copies[-1].start()
    for copy in copies:
        copy.wait()


def finished(own, got):
    out = None
    for g, panels in enumerate(GROUPS):
        known = tuple(range(panels[-1] + 1))
        operands = [*own[: g + 1], *got[: g + 1]] + ([] if out is None else [out])
        copies = sum(j + 1 for j in panels)
        out = pl.pallas_call(
            functools.partial(finish_kernel, panels, known, g + 1),
            out_shape=jax.ShapeDtypeStruct((FRAMES, FRAMES), jnp.float32),
            in_specs=[VMEM] * (2 * g + 2) + ([] if out is None else [ANY]),
            out_specs=ANY,
            input_output_aliases={} if out is None else {2 * g + 2: 0},
            scratch_shapes=[
                pltpu.VMEM((FRAMES, FRAMES), jnp.float32),
                pltpu.VMEM((FRAMES, FRAMES), jnp.float32),
                pltpu.SemaphoreType.DMA((copies,)),
            ],
            compiler_params=pltpu.CompilerParams(vmem_limit_bytes=12 << 20),
            cost_estimate=pl.CostEstimate(
                flops=8 << 20, bytes_accessed=4 * TILE * TILE * copies * 2, transcendentals=0
            ),
            name="finish",
        )(*operands)
    return out


def local(intensity, block_annulus):
    devices = lax.axis_size("sector") * lax.axis_size("frame")
    pieces = intensity.reshape(4, devices, BLOCKS, 128).transpose(1, 2, 0, 3)
    arrived = lax.all_to_all(pieces, ("sector", "frame"), split_axis=0, concat_axis=0, tiled=True)
    arrived = arrived.reshape(4, devices // 4, BLOCKS // QUAD, 4 * QUAD, 128)
    return after(arrived, block_annulus)


def after(arrived, block_annulus):
    pairs = [(source, source ^ 1) for source in range(lax.axis_size("frame"))]
    own, got, pixels = [], [], arrived
    for panels in GROUPS:
        mine, other, *in_order = packed_grams(panels, block_annulus, pixels)
        pixels = in_order[0] if in_order else pixels
        own.append(mine)
        got.append(lax.ppermute(other, "frame", pairs))
    return finished(own, got).reshape(1, 1, FRAMES, FRAMES)


def solution(mesh):
    in_specs = (P(("frame", "sector"), None), P("sector", "frame"))
    out_specs = P("sector", "frame", None, None)
    return jax.shard_map(local, mesh=mesh, in_specs=in_specs, out_specs=out_specs, check_vma=False)
```

```python
import functools

import jax
import jax.numpy as jnp
from jax import lax
from jax.experimental import pallas as pl
from jax.experimental.pallas import tpu as pltpu
from jax.sharding import PartitionSpec as P

FRAMES = 1024
TILE = 256
PARTS = FRAMES // TILE
HEAD = 16
BLOCKS = 24
QUAD = 4
WIDTH = 128 * QUAD
QUADS = BLOCKS // QUAD
SLOTS = QUADS + 1
GROUP = 2
GROUPS = ((0, 1, 2), (3,))
VMEM = pl.BlockSpec(memory_space=pltpu.VMEM)
SMEM = pl.BlockSpec(memory_space=pltpu.SMEM)
ANY = pl.BlockSpec(memory_space=pl.ANY)


def starts_of(panels):
    starts, row = {}, 0
    for j in panels:
        starts[j] = row
        row += HEAD + TILE * (j + 1)
    return starts, row


def put_in_order(landed, ordered, slot, quad):
    low = lax.broadcasted_iota(jnp.int32, (GROUP, 8, 128), 1) < 4
    for g in range(FRAMES // 16 // GROUP):
        tiles = [
            landed[s, GROUP * g : GROUP * g + GROUP, quad].astype(jnp.float32) for s in range(4)
        ]
        for b in range(QUAD):
            here = [tile[:, 8 * (b // 2) : 8 * (b // 2) + 8] for tile in tiles]
            moved = [pltpu.roll(part, 4, 1) for part in here]
            first, second = (moved, here) if b % 2 else (here, moved)
            halves = [jnp.where(low, first[s], second[s + 1]) for s in (0, 2)]
            block = jnp.concatenate(halves, axis=1).astype(jnp.bfloat16)
            lane = pl.multiple_of(WIDTH * slot + 128 * b, 128)
            row = HEAD + 16 * GROUP * g
            ordered[row : row + 16 * GROUP, pl.ds(lane, 128)] = block.reshape(16 * GROUP, 128)


def gram_kernel(panels, arrives, annulus_ref, *refs):
    if arrives:
        landed, own_ref, other_ref, ordered = refs
    else:
        ordered, own_ref, other_ref = refs
    starts, _ = starts_of(panels)
    number = lax.axis_index("sector") * lax.axis_size("frame") + lax.axis_index("frame")

    def flag(block):
        return jnp.where(annulus_ref[0, block] == number, 1, 0)

    own_blocks = flag(0)
    for b in range(1, BLOCKS):
        own_blocks += flag(b)
    last = (own_blocks + QUAD - 1) // QUAD - 1

    def quad_of(near):
        return jnp.where(number % 2 == 0, near, QUADS - 1 - near)

    if arrives:
        ordered[0:HEAD] = jnp.ones((HEAD, WIDTH * SLOTS), jnp.bfloat16)

        def fill(near, carry):
            slot = jnp.where(near <= last, near, near + 1)
            put_in_order(landed, ordered, slot, quad_of(near))
            return carry

        lax.fori_loop(0, QUADS, fill, 0)
        shared = pl.multiple_of(WIDTH * last, WIDTH)
        after = pl.multiple_of(shared + WIDTH, WIDTH)
        ordered[HEAD:, pl.ds(after, WIDTH)] = ordered[HEAD:, pl.ds(shared, WIDTH)]
        for b in range(QUAD):
            mine = flag(QUAD * quad_of(last) + b)
            lane = pl.multiple_of(jnp.where(mine == 1, after, shared) + 128 * b, 128)
            ordered[HEAD:, pl.ds(lane, 128)] = jnp.zeros((FRAMES, 128), jnp.bfloat16)

    def products(out_ref, low, high):
        for j in panels:
            rows = HEAD + TILE * (j + 1)
            out_ref[starts[j] : starts[j] + rows] = lax.dot_general(
                ordered[0:rows, WIDTH * low : WIDTH * high],
                ordered[HEAD + TILE * j : HEAD + TILE * j + TILE, WIDTH * low : WIDTH * high],
                (((1,), (1,)), ((), ())),
                preferred_element_type=jnp.float32,
            )

    for end in range(QUADS):

        @pl.when(last == end)
        def _(end=end):
            products(own_ref, 0, end + 1)
            products(other_ref, end + 1, SLOTS)

    count = 128.0 * own_blocks.astype(jnp.float32)
    own_ref[8:16] = jnp.full((8, TILE), count, jnp.float32)
    other_ref[8:16] = jnp.full((8, TILE), 128.0 * BLOCKS - count, jnp.float32)


def packed_grams(panels, block_annulus, operand):
    arrives = operand.ndim == 5
    packed = jax.ShapeDtypeStruct((starts_of(panels)[1], TILE), jnp.float32)
    in_order = jax.ShapeDtypeStruct((HEAD + FRAMES, WIDTH * SLOTS), jnp.bfloat16)
    out_shape = (packed, packed, in_order) if arrives else (packed, packed)
    return pl.pallas_call(
        functools.partial(gram_kernel, panels, arrives),
        out_shape=out_shape,
        in_specs=[SMEM, VMEM],
        out_specs=(VMEM,) * len(out_shape),
        compiler_params=pltpu.CompilerParams(vmem_limit_bytes=24 << 20),
        cost_estimate=pl.CostEstimate(
            flops=2 * packed.size * WIDTH * SLOTS, bytes_accessed=6 << 20, transcendentals=0
        ),
        name="grams",
    )(block_annulus, operand)


def finish_kernel(panels, known, groups, *refs):
    own_refs, got_refs, refs = refs[:groups], refs[groups : 2 * groups], refs[2 * groups :]
    out_ref, blocks, copied = refs[-3:]
    place = {
        j: (own_refs[g], got_refs[g], starts_of(GROUPS[g])[0][j])
        for g in range(groups)
        for j in GROUPS[g]
    }

    def total(j, row, rows):
        own_ref, got_ref, start = place[j]
        return own_ref[start + row : start + row + rows] + got_ref[start + row : start + row + rows]

    inverse = {j: 1.0 / total(j, 0, 8)[0:1] for j in known}
    count = total(0, 8, 8)[0:1]

    def column(j):
        half = [
            jnp.transpose(jnp.broadcast_to(inverse[j][:, 128 * k : 128 * k + 128], (128, 128)))
            for k in range(TILE // 128)
        ]
        half = jnp.concatenate(half, axis=0)
        return jnp.concatenate([half, half], axis=1)

    left = {j: column(j) for j in known}
    copies = []

    def send(source_ref, i, j, block):
        rows, columns = slice(TILE * i, TILE * i + TILE), slice(TILE * j, TILE * j + TILE)
        source_ref[rows, columns] = block
        copies.append(
            pltpu.make_async_copy(
                source_ref.at[rows, columns], out_ref.at[rows, columns], copied.at[len(copies)]
            )
        )
        copies[-1].start()

    for j in panels:
        for i in range(j + 1):
            block = total(j, HEAD + TILE * i, TILE) * left[i] * (count * inverse[j])
            send(blocks, i, j, block)
            if i < j:
                send(blocks, j, i, jnp.transpose(block))
    for copy in copies:
        copy.wait()


def finished(own, got):
    out = None
    for g, panels in enumerate(GROUPS):
        known = tuple(range(panels[-1] + 1))
        operands = [*own[: g + 1], *got[: g + 1]] + ([] if out is None else [out])
        copies = sum(2 * j + 1 for j in panels)
        out = pl.pallas_call(
            functools.partial(finish_kernel, panels, known, g + 1),
            out_shape=jax.ShapeDtypeStruct((FRAMES, FRAMES), jnp.float32),
            in_specs=[VMEM] * (2 * g + 2) + ([] if out is None else [ANY]),
            out_specs=ANY,
            input_output_aliases={} if out is None else {2 * g + 2: 0},
            scratch_shapes=[
                pltpu.VMEM((FRAMES, FRAMES), jnp.float32),
                pltpu.SemaphoreType.DMA((copies,)),
            ],
            compiler_params=pltpu.CompilerParams(vmem_limit_bytes=12 << 20),
            cost_estimate=pl.CostEstimate(
                flops=8 << 20, bytes_accessed=4 * TILE * TILE * copies, transcendentals=0
            ),
            name="finish",
        )(*operands)
    return out


def local(intensity, block_annulus):
    devices = lax.axis_size("sector") * lax.axis_size("frame")
    pieces = intensity.reshape(4, devices, BLOCKS, 128).transpose(1, 2, 0, 3)
    arrived = lax.all_to_all(pieces, ("sector", "frame"), split_axis=0, concat_axis=0, tiled=True)
    arrived = arrived.reshape(4, devices // 4, BLOCKS // QUAD, 4 * QUAD, 128)
    return after(arrived, block_annulus)


def after(arrived, block_annulus):
    pairs = [(source, source ^ 1) for source in range(lax.axis_size("frame"))]
    own, got, pixels = [], [], arrived
    for panels in GROUPS:
        mine, other, *in_order = packed_grams(panels, block_annulus, pixels)
        pixels = in_order[0] if in_order else pixels
        own.append(mine)
        got.append(lax.ppermute(other, "frame", pairs))
    return finished(own, got).reshape(1, 1, FRAMES, FRAMES)


def solution(mesh):
    in_specs = (P(("frame", "sector"), None), P("sector", "frame"))
    out_specs = P("sector", "frame", None, None)
    return jax.shard_map(local, mesh=mesh, in_specs=in_specs, out_specs=out_specs, check_vma=False)
```

```python
import functools

import jax
import jax.numpy as jnp
from jax import lax
from jax.experimental import pallas as pl
from jax.experimental.pallas import tpu as pltpu
from jax.sharding import PartitionSpec as P

FRAMES = 1024
TILE = 256
PARTS = FRAMES // TILE
HEAD = 16
BLOCKS = 24
QUAD = 4
WIDTH = 128 * QUAD
QUADS = BLOCKS // QUAD
SLOTS = QUADS + 1
GROUP = 2
GROUPS = ((0, 1, 2), (3,))
VMEM = pl.BlockSpec(memory_space=pltpu.VMEM)
ANY = pl.BlockSpec(memory_space=pl.ANY)


def starts_of(panels):
    starts, row = {}, 0
    for j in panels:
        starts[j] = row
        row += HEAD + TILE * (j + 1)
    return starts, row


def put_in_order(landed, ordered, slot, quad):
    low = lax.broadcasted_iota(jnp.int32, (GROUP, 8, 128), 1) < 4
    for g in range(FRAMES // 16 // GROUP):
        tiles = [
            landed[s, GROUP * g : GROUP * g + GROUP, quad].astype(jnp.float32) for s in range(4)
        ]
        for b in range(QUAD):
            here = [tile[:, 8 * (b // 2) : 8 * (b // 2) + 8] for tile in tiles]
            moved = [pltpu.roll(part, 4, 1) for part in here]
            first, second = (moved, here) if b % 2 else (here, moved)
            halves = [jnp.where(low, first[s], second[s + 1]) for s in (0, 2)]
            block = jnp.concatenate(halves, axis=1).astype(jnp.bfloat16)
            lane = pl.multiple_of(WIDTH * slot + 128 * b, 128)
            row = HEAD + 16 * GROUP * g
            ordered[row : row + 16 * GROUP, pl.ds(lane, 128)] = block.reshape(16 * GROUP, 128)


def gram_kernel(panels, arrives, annulus_ref, *refs):
    if arrives:
        landed, own_ref, other_ref, ordered = refs
    else:
        ordered, own_ref, other_ref = refs
    starts, _ = starts_of(panels)
    number = lax.axis_index("sector") * lax.axis_size("frame") + lax.axis_index("frame")

    own_blocks = jnp.sum(jnp.where(annulus_ref[...] == number, 1.0, 0.0)).astype(jnp.int32)
    last = (own_blocks + QUAD - 1) // QUAD - 1

    def quad_of(near):
        return jnp.where(number % 2 == 0, near, QUADS - 1 - near)

    if arrives:
        ordered[0:HEAD] = jnp.ones((HEAD, WIDTH * SLOTS), jnp.bfloat16)

        for near in range(QUADS):
            slot = jnp.where(near <= last, near, near + 1) if near else 0
            put_in_order(landed, ordered, slot, quad_of(near))

    def split(end):
        shared, after = WIDTH * end, WIDTH * (end + 1)
        ordered[HEAD:, after : after + WIDTH] = ordered[HEAD:, shared : shared + WIDTH]
        for b in range(QUAD):
            place = QUAD * end + jnp.where(number % 2 == 0, b, QUAD - 1 - b)
            lane = pl.multiple_of(jnp.where(place < own_blocks, after, shared) + 128 * b, 128)
            ordered[HEAD:, pl.ds(lane, 128)] = jnp.zeros((FRAMES, 128), jnp.bfloat16)

    def products(out_ref, low, high):
        for j in panels:
            rows = HEAD + TILE * (j + 1)
            out_ref[starts[j] : starts[j] + rows] = lax.dot_general(
                ordered[0:rows, WIDTH * low : WIDTH * high],
                ordered[HEAD + TILE * j : HEAD + TILE * j + TILE, WIDTH * low : WIDTH * high],
                (((1,), (1,)), ((), ())),
                preferred_element_type=jnp.float32,
            )

    for end in range(QUADS):

        @pl.when(last == end)
        def _(end=end):
            if arrives:
                split(end)
            products(own_ref, 0, end + 1)
            products(other_ref, end + 1, SLOTS)

    count = 128.0 * own_blocks.astype(jnp.float32)
    own_ref[8:16] = jnp.full((8, TILE), count, jnp.float32)
    other_ref[8:16] = jnp.full((8, TILE), 128.0 * BLOCKS - count, jnp.float32)


def packed_grams(panels, block_annulus, operand):
    arrives = operand.ndim == 5
    packed = jax.ShapeDtypeStruct((starts_of(panels)[1], TILE), jnp.float32)
    in_order = jax.ShapeDtypeStruct((HEAD + FRAMES, WIDTH * SLOTS), jnp.bfloat16)
    out_shape = (packed, packed, in_order) if arrives else (packed, packed)
    return pl.pallas_call(
        functools.partial(gram_kernel, panels, arrives),
        out_shape=out_shape,
        in_specs=[VMEM, VMEM],
        out_specs=(VMEM,) * len(out_shape),
        compiler_params=pltpu.CompilerParams(vmem_limit_bytes=24 << 20),
        cost_estimate=pl.CostEstimate(
            flops=2 * packed.size * WIDTH * SLOTS, bytes_accessed=6 << 20, transcendentals=0
        ),
        name="grams",
    )(block_annulus, operand)


def finish_kernel(panels, known, groups, *refs):
    own_refs, got_refs, refs = refs[:groups], refs[groups : 2 * groups], refs[2 * groups :]
    out_ref, blocks, copied = refs[-3:]
    place = {
        j: (own_refs[g], got_refs[g], starts_of(GROUPS[g])[0][j])
        for g in range(groups)
        for j in GROUPS[g]
    }

    def total(j, row, rows):
        own_ref, got_ref, start = place[j]
        return own_ref[start + row : start + row + rows] + got_ref[start + row : start + row + rows]

    inverse = {j: 1.0 / total(j, 0, 8)[0:1] for j in known}
    count = total(0, 8, 8)[0:1]

    def column(j):
        half = [
            jnp.transpose(jnp.broadcast_to(inverse[j][:, 128 * k : 128 * k + 128], (128, 128)))
            for k in range(TILE // 128)
        ]
        half = jnp.concatenate(half, axis=0)
        return jnp.concatenate([half, half], axis=1)

    left = {j: column(j) for j in known}
    copies = []

    def send(source_ref, i, j, block):
        rows, columns = slice(TILE * i, TILE * i + TILE), slice(TILE * j, TILE * j + TILE)
        source_ref[rows, columns] = block
        copies.append(
            pltpu.make_async_copy(
                source_ref.at[rows, columns], out_ref.at[rows, columns], copied.at[len(copies)]
            )
        )
        copies[-1].start()

    for j in panels:
        for i in range(j + 1):
            block = total(j, HEAD + TILE * i, TILE) * left[i] * (count * inverse[j])
            send(blocks, i, j, block)
            if i < j:
                send(blocks, j, i, jnp.transpose(block))
    for copy in copies:
        copy.wait()


def finished(own, got):
    out = None
    for g, panels in enumerate(GROUPS):
        known = tuple(range(panels[-1] + 1))
        operands = [*own[: g + 1], *got[: g + 1]] + ([] if out is None else [out])
        copies = sum(2 * j + 1 for j in panels)
        out = pl.pallas_call(
            functools.partial(finish_kernel, panels, known, g + 1),
            out_shape=jax.ShapeDtypeStruct((FRAMES, FRAMES), jnp.float32),
            in_specs=[VMEM] * (2 * g + 2) + ([] if out is None else [ANY]),
            out_specs=ANY,
            input_output_aliases={} if out is None else {2 * g + 2: 0},
            scratch_shapes=[
                pltpu.VMEM((FRAMES, FRAMES), jnp.float32),
                pltpu.SemaphoreType.DMA((copies,)),
            ],
            compiler_params=pltpu.CompilerParams(vmem_limit_bytes=12 << 20),
            cost_estimate=pl.CostEstimate(
                flops=8 << 20, bytes_accessed=4 * TILE * TILE * copies, transcendentals=0
            ),
            name="finish",
        )(*operands)
    return out


def local(intensity, block_annulus):
    devices = lax.axis_size("sector") * lax.axis_size("frame")
    pieces = intensity.reshape(4, devices, BLOCKS, 128).transpose(1, 2, 0, 3)
    arrived = lax.all_to_all(pieces, ("sector", "frame"), split_axis=0, concat_axis=0, tiled=True)
    arrived = arrived.reshape(4, devices // 4, BLOCKS // QUAD, 4 * QUAD, 128)
    return after(arrived, block_annulus)


def after(arrived, block_annulus):
    pairs = [(source, source ^ 1) for source in range(lax.axis_size("frame"))]
    own, got, pixels = [], [], arrived
    for panels in GROUPS:
        mine, other, *in_order = packed_grams(panels, block_annulus, pixels)
        pixels = in_order[0] if in_order else pixels
        own.append(mine)
        got.append(lax.ppermute(other, "frame", pairs))
    return finished(own, got).reshape(1, 1, FRAMES, FRAMES)


def solution(mesh):
    in_specs = (P(("frame", "sector"), None), P("sector", "frame"))
    out_specs = P("sector", "frame", None, None)
    return jax.shard_map(local, mesh=mesh, in_specs=in_specs, out_specs=out_specs, check_vma=False)
```

```python
import functools

import jax
import jax.numpy as jnp
from jax import lax
from jax.experimental import pallas as pl
from jax.experimental.pallas import tpu as pltpu
from jax.sharding import PartitionSpec as P

FRAMES = 1024
TILE = 256
PARTS = FRAMES // TILE
HEAD = 16
SUMS = 8
HALF = TILE // 2
BLOCKS = 24
QUAD = 4
WIDTH = 128 * QUAD
QUADS = BLOCKS // QUAD
SLOTS = QUADS + 1
GROUP = 2
GROUPS = ((0, 1, 2), (3,))
VMEM = pl.BlockSpec(memory_space=pltpu.VMEM)
ANY = pl.BlockSpec(memory_space=pl.ANY)


def starts_of(panels):
    starts, row = {}, 0
    for j in panels:
        starts[j] = row
        row += SUMS + TILE * j + TILE * 3 // 4
    return starts, row


def put_in_order(landed, ordered, slot, quad):
    low = lax.broadcasted_iota(jnp.int32, (GROUP, 8, 128), 1) < 4
    for g in range(FRAMES // 16 // GROUP):
        tiles = [
            landed[s, GROUP * g : GROUP * g + GROUP, quad].astype(jnp.float32) for s in range(4)
        ]
        for b in range(QUAD):
            here = [tile[:, 8 * (b // 2) : 8 * (b // 2) + 8] for tile in tiles]
            moved = [pltpu.roll(part, 4, 1) for part in here]
            first, second = (moved, here) if b % 2 else (here, moved)
            halves = [jnp.where(low, first[s], second[s + 1]) for s in (0, 2)]
            block = jnp.concatenate(halves, axis=1).astype(jnp.bfloat16)
            lane = pl.multiple_of(WIDTH * slot + 128 * b, 128)
            row = HEAD + 16 * GROUP * g
            ordered[row : row + 16 * GROUP, pl.ds(lane, 128)] = block.reshape(16 * GROUP, 128)


def gram_kernel(panels, arrives, annulus_ref, *refs):
    if arrives:
        landed, own_ref, other_ref, ordered = refs
    else:
        ordered, own_ref, other_ref = refs
    starts, _ = starts_of(panels)
    number = lax.axis_index("sector") * lax.axis_size("frame") + lax.axis_index("frame")

    own_blocks = jnp.sum(jnp.where(annulus_ref[...] == number, 1.0, 0.0)).astype(jnp.int32)
    last = (own_blocks + QUAD - 1) // QUAD - 1

    def quad_of(near):
        return jnp.where(number % 2 == 0, near, QUADS - 1 - near)

    if arrives:
        ordered[0:HEAD] = jnp.ones((HEAD, WIDTH * SLOTS), jnp.bfloat16)

        for near in range(QUADS):
            slot = jnp.where(near <= last, near, near + 1) if near else 0
            put_in_order(landed, ordered, slot, quad_of(near))

    def split(end):
        shared, after = WIDTH * end, WIDTH * (end + 1)
        ordered[HEAD:, after : after + WIDTH] = ordered[HEAD:, shared : shared + WIDTH]
        for b in range(QUAD):
            place = QUAD * end + jnp.where(number % 2 == 0, b, QUAD - 1 - b)
            lane = pl.multiple_of(jnp.where(place < own_blocks, after, shared) + 128 * b, 128)
            ordered[HEAD:, pl.ds(lane, 128)] = jnp.zeros((FRAMES, 128), jnp.bfloat16)

    def products(out_ref, low, high):
        for j in panels:
            rows = HEAD + TILE * (j + 1)
            panel = lax.dot_general(
                ordered[0:rows, WIDTH * low : WIDTH * high],
                ordered[HEAD + TILE * j : HEAD + TILE * j + TILE, WIDTH * low : WIDTH * high],
                (((1,), (1,)), ((), ())),
                preferred_element_type=jnp.float32,
            )
            folded = starts[j] + SUMS + TILE * j + HALF
            out_ref[starts[j] : folded] = panel[HEAD - SUMS : rows - HALF]
            for k in range(2):
                out_ref[folded : folded + HALF // 2, HALF * k : HALF * k + HALF] = panel[
                    rows - HALF + HALF // 2 * k : rows - HALF + HALF // 2 * (k + 1), HALF:
                ]

    for end in range(QUADS):

        @pl.when(last == end)
        def _(end=end):
            if arrives:
                split(end)
            products(own_ref, 0, end + 1)
            products(other_ref, end + 1, SLOTS)

    count = 128.0 * own_blocks.astype(jnp.float32)
    own_ref[SUMS - 1 : SUMS] = jnp.full((1, TILE), count, jnp.float32)
    other_ref[SUMS - 1 : SUMS] = jnp.full((1, TILE), 128.0 * BLOCKS - count, jnp.float32)


def packed_grams(panels, block_annulus, operand):
    arrives = operand.ndim == 5
    packed = jax.ShapeDtypeStruct((starts_of(panels)[1], TILE), jnp.float32)
    in_order = jax.ShapeDtypeStruct((HEAD + FRAMES, WIDTH * SLOTS), jnp.bfloat16)
    out_shape = (packed, packed, in_order) if arrives else (packed, packed)
    return pl.pallas_call(
        functools.partial(gram_kernel, panels, arrives),
        out_shape=out_shape,
        in_specs=[VMEM, VMEM],
        out_specs=(VMEM,) * len(out_shape),
        compiler_params=pltpu.CompilerParams(vmem_limit_bytes=24 << 20),
        cost_estimate=pl.CostEstimate(
            flops=2 * packed.size * WIDTH * SLOTS, bytes_accessed=6 << 20, transcendentals=0
        ),
        name="grams",
    )(block_annulus, operand)


def finish_kernel(panels, known, groups, *refs):
    own_refs, got_refs, refs = refs[:groups], refs[groups : 2 * groups], refs[2 * groups :]
    out_ref, blocks, copied = refs[-3:]
    place = {
        j: (own_refs[g], got_refs[g], starts_of(GROUPS[g])[0][j])
        for g in range(groups)
        for j in GROUPS[g]
    }

    def total(j, row, rows):
        own_ref, got_ref, start = place[j]
        return own_ref[start + row : start + row + rows] + got_ref[start + row : start + row + rows]

    inverse = {j: 1.0 / total(j, 0, 1) for j in known}
    count = total(0, SUMS - 1, 1)

    def column(j):
        half = [
            jnp.transpose(jnp.broadcast_to(inverse[j][:, 128 * k : 128 * k + 128], (128, 128)))
            for k in range(TILE // 128)
        ]
        half = jnp.concatenate(half, axis=0)
        return jnp.concatenate([half, half], axis=1)

    left = {j: column(j) for j in known}
    copies = []

    def send(source_ref, i, j, block):
        rows, columns = slice(TILE * i, TILE * i + TILE), slice(TILE * j, TILE * j + TILE)
        source_ref[rows, columns] = block
        copies.append(
            pltpu.make_async_copy(
                source_ref.at[rows, columns], out_ref.at[rows, columns], copied.at[len(copies)]
            )
        )
        copies[-1].start()

    def products(i, j):
        if i < j:
            return total(j, SUMS + TILE * i, TILE)
        upper = total(j, SUMS + TILE * j, HALF)
        folded = total(j, SUMS + TILE * j + HALF, HALF // 2)
        right = jnp.concatenate([folded[:, :HALF], folded[:, HALF:]], axis=0)
        lower = jnp.concatenate([jnp.transpose(upper[:, HALF:]), right], axis=1)
        return jnp.concatenate([upper, lower], axis=0)

    for j in panels:
        for i in range(j + 1):
            block = products(i, j) * left[i] * (count * inverse[j])
            send(blocks, i, j, block)
            if i < j:
                send(blocks, j, i, jnp.transpose(block))
    for copy in copies:
        copy.wait()


def finished(own, got):
    out = None
    for g, panels in enumerate(GROUPS):
        known = tuple(range(panels[-1] + 1))
        operands = [*own[: g + 1], *got[: g + 1]] + ([] if out is None else [out])
        copies = sum(2 * j + 1 for j in panels)
        out = pl.pallas_call(
            functools.partial(finish_kernel, panels, known, g + 1),
            out_shape=jax.ShapeDtypeStruct((FRAMES, FRAMES), jnp.float32),
            in_specs=[VMEM] * (2 * g + 2) + ([] if out is None else [ANY]),
            out_specs=ANY,
            input_output_aliases={} if out is None else {2 * g + 2: 0},
            scratch_shapes=[
                pltpu.VMEM((FRAMES, FRAMES), jnp.float32),
                pltpu.SemaphoreType.DMA((copies,)),
            ],
            compiler_params=pltpu.CompilerParams(vmem_limit_bytes=12 << 20),
            cost_estimate=pl.CostEstimate(
                flops=8 << 20, bytes_accessed=4 * TILE * TILE * copies, transcendentals=0
            ),
            name="finish",
        )(*operands)
    return out


def local(intensity, block_annulus):
    devices = lax.axis_size("sector") * lax.axis_size("frame")
    pieces = intensity.reshape(4, devices, BLOCKS, 128).transpose(1, 2, 0, 3)
    arrived = lax.all_to_all(pieces, ("sector", "frame"), split_axis=0, concat_axis=0, tiled=True)
    arrived = arrived.reshape(4, devices // 4, BLOCKS // QUAD, 4 * QUAD, 128)
    return after(arrived, block_annulus)


def after(arrived, block_annulus):
    pairs = [(source, source ^ 1) for source in range(lax.axis_size("frame"))]
    own, got, pixels = [], [], arrived
    for panels in GROUPS:
        mine, other, *in_order = packed_grams(panels, block_annulus, pixels)
        pixels = in_order[0] if in_order else pixels
        own.append(mine)
        got.append(lax.ppermute(other, "frame", pairs))
    return finished(own, got).reshape(1, 1, FRAMES, FRAMES)


def solution(mesh):
    in_specs = (P(("frame", "sector"), None), P("sector", "frame"))
    out_specs = P("sector", "frame", None, None)
    return jax.shard_map(local, mesh=mesh, in_specs=in_specs, out_specs=out_specs, check_vma=False)
```
